32 devices in a mesh: round: 4 (over y, x), bucket: 8 (over z, core).
Axes of the slice: x: 2, y: 2, z: 4, core: 2. Of those that a mesh axis runs over, the one named last changes fastest.
Arguments:
- x_start: float32 [4, 4096, 512], P('round', 'bucket'), may hold values from 0 to 1
- y_start: float32 [4, 4096, 512], P('round', 'bucket'), may hold values from 0 to 1
- bucket_payoff: bfloat16 [4, 4096, 4096], P('round', 'bucket'), may hold values from -0.09375 to 0.09375
- column_blocks: int32 [4, 4, 3], P('round'), may hold values from 0 to 3
- public_coef: float32 [4, 4, 3, 128, 128], P('round'), may hold values from -0.3125 to 0.3125
- predecessor_sequences: int32 [3, 256], replicated, may hold values from 0 to 511, as said below
Outputs:
- x_final: float32 [4, 4096, 512], P('round', 'bucket')
- y_final: float32 [4, 4096, 512], P('round', 'bucket')
The draws below stay inside these ranges and needn't reach their ends.
Inputs may be any that keep to these rules, and one draw needn't show every extreme that they name: `predecessor_sequences`: each row names 256 distinct sequences of the previous round.
All inputs are finite; a program needn't handle non-finite values.
Results may differ from the reference program's by a relative error of at most 0.013.
The reference program's roundings to bfloat16 on the way (of `mixed_y` and `mixed_x`) count: a program that leaves them out, or rounds other values in their place, can miss the bound.
Values may be sent and summed in bfloat16 or wider, within the bound.
A program may use at most 64 MiB of HBM per device.

```python
import jax
import jax.numpy as jnp
from jax import lax

K = 4096
S = 512
PB = 128
NBR = 3
ROUNDS = 4
SB = 4
HALF = 256


def draw_predecessor_sequences(key, part):
    row_keys = jax.random.split(key, ROUNDS - 1)

    def one_row(row_key):
        return jax.random.permutation(row_key, S)[:HALF]
    return jax.vmap(one_row)(row_keys).astype(jnp.int32)


def with_ends(values, stream_key, least, largest):
    place = [jax.random.randint(jax.random.fold_in(stream_key, axis), (), 0, length) for axis, length in enumerate(values.shape)]
    main_axis = values.shape.index(max(values.shape))
    beside = place[:main_axis] + [(place[main_axis] + 1) % values.shape[main_axis]] + place[main_axis + 1:]
    return values.at[tuple(place)].set(least).at[tuple(beside)].set(largest)


def shard_levels(key, extent, shards, low, top_value):
    def one(dim, parts):
        draws = jax.random.uniform(jax.random.fold_in(jax.random.fold_in(key, 6), dim), (parts,), jnp.float32, low / len(shards), top_value / len(shards))
        return jnp.repeat(jnp.exp(draws), extent[dim] // parts).reshape((-1,) + (1,) * (len(extent) - dim - 1))

    gain = one(*shards[0])
    for cut in shards[1:]:
        gain = gain * one(*cut)
    return gain


def normal_values(rng, shape, width, reach, pieces=(), kind=jnp.bfloat16):
    factor_of = shard_levels(rng, shape, pieces, -0.22, 0.18) if pieces else 1.0
    result = jax.random.normal(rng, shape, jnp.float32) * width * factor_of
    return jnp.minimum(jnp.maximum(result, -reach), reach).astype(kind)


def setup_inputs(seed: int = 0) -> dict:
    key_list = jax.random.split(jax.random.key(seed), 7)
    x_start = jnp.clip(1.0 * jax.random.uniform(key_list[0], (ROUNDS, K, S), jnp.float32) ** shard_levels(key_list[0], (ROUNDS, K, S), ((0, 4), (1, 8)), -0.2, 0.2), 0.0, 1.0)
    y_start = jnp.clip(1.0 * jax.random.uniform(key_list[1], (ROUNDS, K, S), jnp.float32) ** shard_levels(key_list[1], (ROUNDS, K, S), ((0, 4), (1, 8)), -0.2, 0.2), 0.0, 1.0)
    bucket_payoff = normal_values(key_list[2], (ROUNDS, K, K), K ** -0.5, 0.09375, ((0, 4), (1, 8)))
    column_blocks = with_ends(jax.random.randint(key_list[3], (ROUNDS, SB, NBR), 0, SB), jax.random.fold_in(key_list[3], 1), 0, SB - 1).astype(jnp.int32)
    public_coef = normal_values(key_list[4], (ROUNDS, SB, NBR, PB, PB), (NBR * PB) ** -0.5, 0.3125, ((0, 4),), jnp.float32)
    predecessor_sequences = draw_predecessor_sequences(jax.random.fold_in(key_list[6], 71), 0)
    return dict(x_start=x_start, y_start=y_start, bucket_payoff=bucket_payoff, column_blocks=column_blocks, public_coef=public_coef, predecessor_sequences=predecessor_sequences)


smooth_x = 0.1
smooth_y = 0.1
epsilon = 1e-06
highest = lax.Precision.HIGHEST

def pair_lse(utility_vector):
    even_part = utility_vector[:, 0::2]
    odd_part = utility_vector[:, 1::2]
    larger = jnp.maximum(even_part, odd_part)
    return larger + jnp.log(jnp.exp(even_part - larger) + jnp.exp(odd_part - larger))

def pair_share(utility_vector, aggregated_normalizers, parent_mass):
    even_part = parent_mass * jnp.exp(utility_vector[:, 0::2] - aggregated_normalizers)
    odd_part = parent_mass * jnp.exp(utility_vector[:, 1::2] - aggregated_normalizers)
    return jnp.stack([even_part, odd_part], axis=-1).reshape(utility_vector.shape)

def nested_entropy_mapping(destination_strategy, entropy_weight, predecessor_sequences):
    round_total = destination_strategy.shape[0]
    pair_count = destination_strategy.shape[2] // 2
    divided_utilities = destination_strategy / entropy_weight
    score_list = [None] * round_total
    total_list = [None] * round_total
    for depth_level in reversed(range(round_total)):
        carried = jnp.zeros_like(divided_utilities[depth_level])
        if depth_level < round_total - 1:
            carried = carried.at[:, predecessor_sequences[depth_level]].set(total_list[depth_level + 1])
        score_list[depth_level] = divided_utilities[depth_level] + carried
        total_list[depth_level] = pair_lse(score_list[depth_level])
    masses = []
    previous = jnp.ones((divided_utilities.shape[1], destination_strategy.shape[2]), dtype=divided_utilities.dtype)
    for depth_level in range(round_total):
        if depth_level == 0:
            parent_rows = jnp.arange(pair_count, dtype=jnp.int32)
        else:
            parent_rows = predecessor_sequences[depth_level - 1]
        previous = pair_share(score_list[depth_level], total_list[depth_level], previous[:, parent_rows])
        masses.append(previous)
    return jnp.stack(masses)

def public_forward(strategy, columns, coefficients):
    tiled = strategy.reshape(strategy.shape[0], columns.shape[0], -1)
    picked = tiled[:, columns, :]
    mixed = jnp.einsum('kmtq,mtpq->kmp', picked, coefficients, precision=highest)
    return mixed.reshape(strategy.shape)

def public_backward(strategy, columns, coefficients):
    tiled = strategy.reshape(strategy.shape[0], columns.shape[0], -1)
    spread = jnp.einsum('kmp,mtpq->kmtq', tiled, coefficients, precision=highest)
    selector = (columns[:, :, None] == jnp.arange(columns.shape[0], dtype=jnp.int32)).astype(strategy.dtype)
    gathered = jnp.einsum('kmtq,mtc->kcq', spread, selector, precision=highest)
    return gathered.reshape(strategy.shape)

def reference(x_start, y_start, bucket_payoff, column_blocks, public_coef, predecessor_sequences):
    first_player = x_start
    second_player = y_start
    for step_index in range(2):
        weight_new = 2.0 / (step_index + 3.0)
        mixed_y = jnp.stack([public_forward(second_player[idx_round], column_blocks[idx_round], public_coef[idx_round]) for idx_round in range(ROUNDS)]).astype(jnp.bfloat16)
        grad_x = jnp.stack([jnp.dot(bucket_payoff[idx_round], mixed_y[idx_round], preferred_element_type=jnp.float32) for idx_round in range(ROUNDS)])
        temp_x = smooth_x * jnp.sqrt(jnp.mean(grad_x * grad_x) + epsilon)
        best_x = nested_entropy_mapping(-grad_x, temp_x, predecessor_sequences)
        first_player = (1.0 - weight_new) * first_player + weight_new * best_x
        mixed_x = jnp.stack([public_backward(first_player[idx_round], column_blocks[idx_round], public_coef[idx_round]) for idx_round in range(ROUNDS)]).astype(jnp.bfloat16)
        grad_y = jnp.stack([lax.dot_general(bucket_payoff[idx_round], mixed_x[idx_round], (((0,), (0,)), ((), ())), preferred_element_type=jnp.float32) for idx_round in range(ROUNDS)])
        temp_y = smooth_y * jnp.sqrt(jnp.mean(grad_y * grad_y) + epsilon)
        best_y = nested_entropy_mapping(grad_y, temp_y, predecessor_sequences)
        second_player = (1.0 - weight_new) * second_player + weight_new * best_y
    return (first_player, second_player)
```

```python
import functools

import jax
import jax.numpy as jnp
from jax import lax
from jax.experimental import pallas as pl
from jax.experimental.pallas import tpu as pltpu
from jax.sharding import PartitionSpec as P

smooth_x = 0.1
smooth_y = 0.1
epsilon = 1e-06
highest = lax.Precision.HIGHEST
nn = (((1,), (0,)), ((), ()))
nt = (((1,), (1,)), ((), ()))


def exact(a, b, dims=nn):
    return lax.dot_general(a, b, dims, precision=highest, preferred_element_type=jnp.float32)


def kernel(
    n_r,
    n_b,
    x_ref,
    y_ref,
    pay_ref,
    col_ref,
    coef_ref,
    pred_ref,
    xo_ref,
    yo_ref,
    xs,
    ys,
    mixer,
    gather,
    pay_t,
    blocks,
    mixed,
    grad,
    sib_out,
    sib_in,
    far_out,
    far_in,
    sq_b,
    sq_r,
    rows_in,
    score,
    norm,
    mass,
    back_in,
    ag_send,
    ag_recv,
    fw_send,
    sib_send,
    sib_recv,
    far_send,
    far_recv,
    sqb_send,
    sqb_recv,
    sqr_send,
    sqr_recv,
    row_send,
    row_recv,
    back_send,
    back_recv,
):
    rows, seqs = xs.shape
    half = seqs // 2
    part = rows // n_r
    pairs = n_b // 2
    me_r = lax.axis_index("round")
    me_b = lax.axis_index("bucket")
    pair = me_b // 2
    core = me_b % 2
    sibling = pair * 2 + 1 - core
    total_count = n_r * n_b * rows * seqs

    def remote(src, dst, send, recv, **where):
        return pltpu.make_async_remote_copy(
            src_ref=src,
            dst_ref=dst,
            send_sem=send,
            recv_sem=recv,
            device_id=where,
            device_id_type=pl.DeviceIdType.MESH,
        )

    barrier = pltpu.get_barrier_semaphore()
    for d in range(1, n_b):
        pl.semaphore_signal(
            barrier,
            inc=1,
            device_id={"bucket": (me_b + d) % n_b},
            device_id_type=pl.DeviceIdType.MESH,
        )
    for d in range(1, n_r):
        pl.semaphore_signal(
            barrier,
            inc=1,
            device_id={"round": (me_r + d) % n_r},
            device_id_type=pl.DeviceIdType.MESH,
        )
    pl.semaphore_wait(barrier, n_b + n_r - 2)

    def order(i):
        return jnp.where(i < half, 2 * i, 2 * (i - half) + 1)

    down = lax.broadcasted_iota(jnp.int32, (seqs, seqs), 0)
    across = lax.broadcasted_iota(jnp.int32, (seqs, seqs), 1)
    to_inner = (down == order(across)).astype(jnp.float32)
    to_outer = (order(down) == across).astype(jnp.float32)

    tiles, per_row, tile, _ = coef_ref.shape[1:]
    for m in range(tiles):
        for c in range(tiles):
            value = jnp.zeros((tile, tile), jnp.float32)
            for t in range(per_row):
                value = value + jnp.where(col_ref[0, m, t] == c, coef_ref[0, m, t], 0.0)
            mixer[m * tile : (m + 1) * tile, c * tile : (c + 1) * tile] = value
    mixer[...] = exact(to_outer, exact(mixer[...], to_inner))
    ys[...] = exact(y_ref[0], to_inner)
    xs[...] = exact(x_ref[0], to_inner)
    for r in range(n_r - 1):
        place = order(lax.broadcasted_iota(jnp.int32, (seqs, half), 0))
        gather[r] = (place == pred_ref[r : r + 1, :]).astype(jnp.float32)

    def columns(j):
        return pl.ds(pl.multiple_of(j * rows, rows), rows)

    def prox(state, sign, factor, weight):
        def row_copy(d):
            s = (me_r + d) % n_r
            return remote(
                grad.at[pl.ds(pl.multiple_of(s * part, part), part)],
                rows_in.at[me_r],
                row_send.at[s],
                row_recv.at[me_r],
                round=s,
            )

        def row_arrival(d):
            s = (me_r + d) % n_r
            return remote(rows_in.at[s], rows_in.at[s], row_send.at[s], row_recv.at[s], round=s)

        for d in range(1, n_r):
            row_copy(d).start()
        squares = grad[...]
        squares = jnp.sum((squares * squares).reshape(rows // 8, 8, seqs), axis=0)
        squares = sum(squares[:, i * 128 : (i + 1) * 128] for i in range(seqs // 128))
        sq_b[me_b] = squares

        def sqb_copy(d):
            s = (me_b + d) % n_b
            return remote(
                sq_b.at[me_b], sq_b.at[me_b], sqb_send.at[d], sqb_recv.at[me_b], bucket=s
            )

        def sqb_arrival(d):
            s = (me_b + d) % n_b
            return remote(sq_b.at[s], sq_b.at[s], sqb_send.at[d], sqb_recv.at[s], bucket=s)

        for d in range(1, n_b):
            sqb_copy(d).start()
        rows_in[me_r] = grad[pl.ds(pl.multiple_of(me_r * part, part), part), :]
        for d in range(1, n_b):
            sqb_arrival(d).wait_recv()
        sq_r[me_r] = jnp.sum(sq_b[...], axis=0)

        def sqr_copy(d):
            s = (me_r + d) % n_r
            return remote(sq_r.at[me_r], sq_r.at[me_r], sqr_send.at[d], sqr_recv.at[me_r], round=s)

        def sqr_arrival(d):
            s = (me_r + d) % n_r
            return remote(sq_r.at[s], sq_r.at[s], sqr_send.at[d], sqr_recv.at[s], round=s)

        for d in range(1, n_r):
            sqr_copy(d).start()
        for d in range(1, n_r):
            sqr_arrival(d).wait_recv()
        squares = jnp.sum(jnp.sum(sq_r[...], axis=0), axis=0, keepdims=True)
        squares = jnp.sum(squares, axis=1, keepdims=True)
        scale = sign / (factor * jnp.sqrt(squares / total_count + epsilon))
        for d in range(1, n_r):
            row_arrival(d).wait_recv()

        for r in reversed(range(n_r)):
            values = rows_in[r] * scale
            if r < n_r - 1:
                values = values + exact(norm[r + 1], gather[r], nt)
            score[r] = values
            even, odd = values[:, :half], values[:, half:]
            larger = jnp.maximum(even, odd)
            norm[r] = larger + jnp.log(jnp.exp(even - larger) + jnp.exp(odd - larger))

        def back_copy(r):
            return remote(
                mass.at[r], back_in.at[me_r], back_send.at[r], back_recv.at[me_r], round=r
            )

        for r in range(n_r):
            even = jnp.exp(score[r, :, :half] - norm[r])
            odd = jnp.exp(score[r, :, half:] - norm[r])
            if r > 0:
                parent = exact(mass[r - 1], gather[r - 1])
                even = parent * even
                odd = parent * odd
            mass[r, :, :half] = even
            mass[r, :, half:] = odd

            @pl.when(me_r != r)
            def _():
                back_copy(r).start()

        def update(s, best):
            here = pl.ds(pl.multiple_of(s * part, part), part)
            state[here, :] = (1.0 - weight) * state[here, :] + weight * best

        update(me_r, mass[me_r])
        for d in range(1, n_r):
            s = (me_r + d) % n_r
            remote(
                back_in.at[s], back_in.at[s], back_send.at[s], back_recv.at[s], round=s
            ).wait_recv()
            update(s, back_in[s])
        for d in range(1, n_r):
            row_copy(d).wait_send()
            back_copy((me_r + d) % n_r).wait_send()
            sqr_copy(d).wait_send()
        for d in range(1, n_b):
            sqb_copy(d).wait_send()

    def step(index, _):
        weight = 2.0 / (index.astype(jnp.float32) + 3.0)

        blocks[me_b] = exact(ys[...], mixer[...], nt).astype(jnp.bfloat16)

        def own_copy(d):
            target = sibling if d == 0 else ((pair + d) % pairs) * 2 + core
            return remote(
                blocks.at[me_b], blocks.at[me_b], ag_send.at[d], ag_recv.at[me_b], bucket=target
            )

        def pass_on(d):
            b = ((pair + d) % pairs) * 2 + core
            return remote(blocks.at[b], blocks.at[b], fw_send.at[d], ag_recv.at[b], bucket=sibling)

        def arrival(b):
            return remote(
                blocks.at[b], blocks.at[b], ag_send.at[0], ag_recv.at[b], bucket=sibling
            )

        def product(b):
            return jnp.dot(
                pay_ref[0, :, columns(b)], blocks[b], preferred_element_type=jnp.float32
            )

        for d in range(1, pairs):
            own_copy(d).start()
        own_copy(0).start()

        @pl.when(index == 0)
        def _():
            def turn(j, _):
                pay_t[columns(j), :] = pay_ref[0, :, columns(j)].T
                return 0

            lax.fori_loop(0, n_b, turn, 0)

        grad[...] = product(me_b)
        arrival(sibling).wait_recv()
        grad[...] += product(sibling)

        def take(d, _):
            b = ((pair + d) % pairs) * 2 + core
            arrival(b).wait_recv()
            pass_on(d).start()
            grad[...] += product(b)
            other = ((pair + d) % pairs) * 2 + 1 - core
            arrival(other).wait_recv()
            grad[...] += product(other)
            return 0

        lax.fori_loop(1, pairs, take, 0)
        own_copy(0).wait_send()
        for d in range(1, pairs):
            own_copy(d).wait_send()
            pass_on(d).wait_send()
        prox(xs, -1.0, smooth_x, weight)

        mixed[...] = exact(xs[...], mixer[...]).astype(jnp.bfloat16)

        def partial(b):
            return jnp.dot(pay_t[columns(b), :], mixed[...], preferred_element_type=jnp.float32)

        def sib_copy(d):
            return remote(
                sib_out.at[d], sib_in.at[d], sib_send.at[d], sib_recv.at[d], bucket=sibling
            )

        def far_copy(d):
            target = ((pair + d) % pairs) * 2 + core
            return remote(
                far_out.at[d], far_in.at[d], far_send.at[d], far_recv.at[d], bucket=target
            )

        def to_sibling(i, _):
            d = pairs - 1 - i
            sib_out[d] = partial(((pair + d) % pairs) * 2 + 1 - core)
            sib_copy(d).start()
            return 0

        lax.fori_loop(0, pairs, to_sibling, 0)

        def to_far(i, _):
            d = pairs - 1 - i
            far_out[d] = partial(((pair + d) % pairs) * 2 + core)
            sib_copy(d).wait_recv()
            far_out[d] += sib_in[d]
            far_copy(d).start()
            return 0

        lax.fori_loop(0, pairs - 1, to_far, 0)
        grad[...] = partial(me_b)
        sib_copy(0).wait_recv()
        grad[...] += sib_in[0]
        for d in range(1, pairs):
            far_copy(d).wait_recv()
            grad[...] += far_in[d]
        sib_copy(0).wait_send()
        for d in range(1, pairs):
            sib_copy(d).wait_send()
            far_copy(d).wait_send()
        prox(ys, 1.0, smooth_y, weight)
        return 0

    lax.fori_loop(0, 2, step, 0)
    down = lax.broadcasted_iota(jnp.int32, (seqs, seqs), 0)
    across = lax.broadcasted_iota(jnp.int32, (seqs, seqs), 1)
    to_outer = (order(down) == across).astype(jnp.float32)
    xo_ref[0] = exact(xs[...], to_outer)
    yo_ref[0] = exact(ys[...], to_outer)


def body(x_start, y_start, bucket_payoff, column_blocks, public_coef, predecessor_sequences):
    n_r = lax.axis_size("round")
    n_b = lax.axis_size("bucket")
    _, rows, seqs = x_start.shape
    part = rows // n_r
    pairs = n_b // 2
    f32, bf16 = jnp.float32, jnp.bfloat16
    vmem = pl.BlockSpec(memory_space=pltpu.VMEM)
    smem = pl.BlockSpec(memory_space=pltpu.SMEM)
    dma = pltpu.SemaphoreType.DMA
    return pl.pallas_call(
        functools.partial(kernel, n_r, n_b),
        out_shape=[jax.ShapeDtypeStruct(x_start.shape, f32)] * 2,
        in_specs=[vmem, vmem, vmem, smem, vmem, vmem],
        out_specs=[vmem, vmem],
        scratch_shapes=[
            pltpu.VMEM((rows, seqs), f32),
            pltpu.VMEM((rows, seqs), f32),
            pltpu.VMEM((seqs, seqs), f32),
            pltpu.VMEM((n_r - 1, seqs, seqs // 2), f32),
            pltpu.VMEM((n_b * rows, rows), bf16),
            pltpu.VMEM((n_b, rows, seqs), bf16),
            pltpu.VMEM((rows, seqs), bf16),
            pltpu.VMEM((rows, seqs), f32),
            pltpu.VMEM((pairs, rows, seqs), f32),
            pltpu.VMEM((pairs, rows, seqs), f32),
            pltpu.VMEM((pairs, rows, seqs), f32),
            pltpu.VMEM((pairs, rows, seqs), f32),
            pltpu.VMEM((n_b, 8, 128), f32),
            pltpu.VMEM((n_r, 8, 128), f32),
            pltpu.VMEM((n_r, part, seqs), f32),
            pltpu.VMEM((n_r, part, seqs), f32),
            pltpu.VMEM((n_r, part, seqs // 2), f32),
            pltpu.VMEM((n_r, part, seqs), f32),
            pltpu.VMEM((n_r, part, seqs), f32),
            dma((pairs,)),
            dma((n_b,)),
            dma((pairs,)),
            dma((pairs,)),
            dma((pairs,)),
            dma((pairs,)),
            dma((pairs,)),
            dma((n_b,)),
            dma((n_b,)),
            dma((n_r,)),
            dma((n_r,)),
            dma((n_r,)),
            dma((n_r,)),
            dma((n_r,)),
            dma((n_r,)),
        ],
        compiler_params=pltpu.CompilerParams(
            collective_id=0, has_side_effects=True, vmem_limit_bytes=60 * 1024 * 1024
        ),
    )(x_start, y_start, bucket_payoff, column_blocks, public_coef, predecessor_sequences)


def solution(mesh):
    in_specs = (
        P("round", "bucket", None),
        P("round", "bucket", None),
        P("round", "bucket", None),
        P("round", None, None),
        P("round", None, None, None, None),
        P(),
    )
    out_specs = (P("round", "bucket", None), P("round", "bucket", None))

    def run(*arrays):
        return tuple(
            jax.shard_map(
                body, mesh=mesh, in_specs=in_specs, out_specs=out_specs, check_vma=False
            )(*arrays)
        )

    return run
```

```python
import functools

import jax
import jax.numpy as jnp
from jax import lax
from jax.experimental import pallas as pl
from jax.experimental.pallas import tpu as pltpu
from jax.sharding import PartitionSpec as P

smooth_x = 0.1
smooth_y = 0.1
epsilon = 1e-06
highest = lax.Precision.HIGHEST
nn = (((1,), (0,)), ((), ()))
nt = (((1,), (1,)), ((), ()))


def exact(a, b, dims=nn):
    return lax.dot_general(a, b, dims, precision=highest, preferred_element_type=jnp.float32)


def kernel(
    n_r,
    n_b,
    x_ref,
    y_ref,
    pay_ref,
    col_ref,
    coef_ref,
    pred_ref,
    xo_ref,
    yo_ref,
    xs,
    ys,
    mixer,
    gather,
    pay_t,
    blocks,
    mixed,
    grad,
    sib_out,
    sib_in,
    far_out,
    far_in,
    sq_b,
    sq_r,
    rows_in,
    score,
    norm,
    mass,
    back_in,
    far_q,
    far_s,
    far_q_in,
    far_s_in,
    row_q,
    row_s,
    row_q_in,
    row_s_in,
    back_q,
    back_s,
    back_q_in,
    back_s_in,
    ag_send,
    ag_recv,
    fw_send,
    line_send,
    sib_send,
    sib_recv,
    far_send,
    far_recv,
    sqb_send,
    sqb_recv,
    sqr_send,
    sqr_recv,
    row_send,
    row_recv,
    back_send,
    back_recv,
    far_s_send,
    far_s_recv,
    row_s_send,
    row_s_recv,
    back_s_send,
    back_s_recv,
):
    rows, seqs = xs.shape
    half = seqs // 2
    part = rows // n_r
    pairs = n_b // 2
    me_r = lax.axis_index("round")
    me_b = lax.axis_index("bucket")
    pair = me_b // 2
    core = me_b % 2
    sibling = pair * 2 + 1 - core
    total_count = n_r * n_b * rows * seqs

    def remote(src, dst, send, recv, **where):
        return pltpu.make_async_remote_copy(
            src_ref=src,
            dst_ref=dst,
            send_sem=send,
            recv_sem=recv,
            device_id=where,
            device_id_type=pl.DeviceIdType.MESH,
        )

    barrier = pltpu.get_barrier_semaphore()
    for d in range(1, n_b):
        pl.semaphore_signal(
            barrier,
            inc=1,
            device_id={"bucket": (me_b + d) % n_b},
            device_id_type=pl.DeviceIdType.MESH,
        )
    for d in range(1, n_r):
        pl.semaphore_signal(
            barrier,
            inc=1,
            device_id={"round": (me_r + d) % n_r},
            device_id_type=pl.DeviceIdType.MESH,
        )
    pl.semaphore_wait(barrier, n_b + n_r - 2)

    def order(i):
        return jnp.where(i < half, 2 * i, 2 * (i - half) + 1)

    down = lax.broadcasted_iota(jnp.int32, (seqs, seqs), 0)
    across = lax.broadcasted_iota(jnp.int32, (seqs, seqs), 1)
    to_inner = (down == order(across)).astype(jnp.float32)
    to_outer = (order(down) == across).astype(jnp.float32)

    tiles, per_row, tile, _ = coef_ref.shape[1:]
    for m in range(tiles):
        for c in range(tiles):
            value = jnp.zeros((tile, tile), jnp.float32)
            for t in range(per_row):
                value = value + jnp.where(col_ref[0, m, t] == c, coef_ref[0, m, t], 0.0)
            mixer[m * tile : (m + 1) * tile, c * tile : (c + 1) * tile] = value
    mixer[...] = exact(to_outer, exact(mixer[...], to_inner))
    ys[...] = exact(y_ref[0], to_inner)
    xs[...] = exact(x_ref[0], to_inner)
    for r in range(n_r - 1):
        place = order(lax.broadcasted_iota(jnp.int32, (seqs, half), 0))
        gather[r] = (place == pred_ref[r : r + 1, :]).astype(jnp.float32)

    def columns(j):
        return pl.ds(pl.multiple_of(j * rows, rows), rows)

    def coded(value, code_ref, scale_ref):
        top = jnp.max(jnp.abs(value), axis=0, keepdims=True)
        unit = jnp.maximum(top, 1e-30) / 32767.0
        code = jnp.floor(value * (1.0 / unit) + 0.5)
        code_ref[...] = code.astype(jnp.int32).astype(jnp.int16)
        scale_ref[...] = jnp.broadcast_to(unit, scale_ref.shape)

    def decoded(code_ref, scale_ref):
        return code_ref[...].astype(jnp.int32).astype(jnp.float32) * scale_ref[0:1, :]

    def prox(state, sign, factor, weight, short):
        def row_copy(d):
            s = (me_r + d) % n_r
            here = grad.at[pl.ds(pl.multiple_of(s * part, part), part)]
            if not short:
                return [
                    remote(here, rows_in.at[me_r], row_send.at[s], row_recv.at[me_r], round=s)
                ]
            return [
                remote(
                    row_q.at[s], row_q_in.at[me_r], row_send.at[s], row_recv.at[me_r], round=s
                ),
                remote(
                    row_s.at[s], row_s_in.at[me_r], row_s_send.at[s], row_s_recv.at[me_r], round=s
                ),
            ]

        def row_arrival(d):
            s = (me_r + d) % n_r
            if not short:
                return [
                    remote(rows_in.at[s], rows_in.at[s], row_send.at[s], row_recv.at[s], round=s)
                ]
            return [
                remote(row_q_in.at[s], row_q_in.at[s], row_send.at[s], row_recv.at[s], round=s),
                remote(
                    row_s_in.at[s], row_s_in.at[s], row_s_send.at[s], row_s_recv.at[s], round=s
                ),
            ]

        for d in range(1, n_r):
            if short:
                s = (me_r + d) % n_r
                here = pl.ds(pl.multiple_of(s * part, part), part)
                coded(grad[here, :], row_q.at[s], row_s.at[s])
            for copy in row_copy(d):
                copy.start()
        squares = grad[...]
        squares = jnp.sum((squares * squares).reshape(rows // 8, 8, seqs), axis=0)
        squares = sum(squares[:, i * 128 : (i + 1) * 128] for i in range(seqs // 128))
        sq_b[me_b] = squares

        def sqb_copy(d):
            s = (me_b + d) % n_b
            return remote(
                sq_b.at[me_b], sq_b.at[me_b], sqb_send.at[d], sqb_recv.at[me_b], bucket=s
            )

        def sqb_arrival(d):
            s = (me_b + d) % n_b
            return remote(sq_b.at[s], sq_b.at[s], sqb_send.at[d], sqb_recv.at[s], bucket=s)

        for d in range(1, n_b):
            sqb_copy(d).start()
        rows_in[me_r] = grad[pl.ds(pl.multiple_of(me_r * part, part), part), :]
        for d in range(1, n_b):
            sqb_arrival(d).wait_recv()
        sq_r[me_r] = jnp.sum(sq_b[...], axis=0)

        def sqr_copy(d):
            s = (me_r + d) % n_r
            return remote(sq_r.at[me_r], sq_r.at[me_r], sqr_send.at[d], sqr_recv.at[me_r], round=s)

        def sqr_arrival(d):
            s = (me_r + d) % n_r
            return remote(sq_r.at[s], sq_r.at[s], sqr_send.at[d], sqr_recv.at[s], round=s)

        for d in range(1, n_r):
            sqr_copy(d).start()
        for d in range(1, n_r):
            sqr_arrival(d).wait_recv()
        squares = jnp.sum(jnp.sum(sq_r[...], axis=0), axis=0, keepdims=True)
        squares = jnp.sum(squares, axis=1, keepdims=True)
        scale = sign / (factor * jnp.sqrt(squares / total_count + epsilon))
        for d in range(1, n_r):
            for copy in row_arrival(d):
                copy.wait_recv()
            if short:
                s = (me_r + d) % n_r
                rows_in[s] = decoded(row_q_in.at[s], row_s_in.at[s])

        for r in reversed(range(n_r)):
            values = rows_in[r] * scale
            if r < n_r - 1:
                values = values + exact(norm[r + 1], gather[r], nt)
            score[r] = values
            even, odd = values[:, :half], values[:, half:]
            larger = jnp.maximum(even, odd)
            norm[r] = larger + jnp.log(jnp.exp(even - larger) + jnp.exp(odd - larger))

        def back_copy(r):
            if not short:
                return [
                    remote(
                        mass.at[r], back_in.at[me_r], back_send.at[r], back_recv.at[me_r], round=r
                    )
                ]
            return [
                remote(
                    back_q.at[r], back_q_in.at[me_r], back_send.at[r], back_recv.at[me_r], round=r
                ),
                remote(
                    back_s.at[r],
                    back_s_in.at[me_r],
                    back_s_send.at[r],
                    back_s_recv.at[me_r],
                    round=r,
                ),
            ]

        def back_arrival(s):
            if not short:
                return [
                    remote(
                        back_in.at[s], back_in.at[s], back_send.at[s], back_recv.at[s], round=s
                    )
                ]
            return [
                remote(
                    back_q_in.at[s], back_q_in.at[s], back_send.at[s], back_recv.at[s], round=s
                ),
                remote(
                    back_s_in.at[s], back_s_in.at[s], back_s_send.at[s], back_s_recv.at[s], round=s
                ),
            ]

        for r in range(n_r):
            even = jnp.exp(score[r, :, :half] - norm[r])
            odd = jnp.exp(score[r, :, half:] - norm[r])
            if r > 0:
                parent = exact(mass[r - 1], gather[r - 1])
                even = parent * even
                odd = parent * odd
            mass[r, :, :half] = even
            mass[r, :, half:] = odd

            @pl.when(me_r != r)
            def _():
                if short:
                    coded(mass[r], back_q.at[r], back_s.at[r])
                for copy in back_copy(r):
                    copy.start()

        def update(s, best):
            here = pl.ds(pl.multiple_of(s * part, part), part)
            state[here, :] = (1.0 - weight) * state[here, :] + weight * best

        update(me_r, mass[me_r])
        for d in range(1, n_r):
            s = (me_r + d) % n_r
            for copy in back_arrival(s):
                copy.wait_recv()
            if short:
                update(s, decoded(back_q_in.at[s], back_s_in.at[s]))
            else:
                update(s, back_in[s])
        for d in range(1, n_r):
            for copy in row_copy(d) + back_copy((me_r + d) % n_r):
                copy.wait_send()
            sqr_copy(d).wait_send()
        for d in range(1, n_b):
            sqb_copy(d).wait_send()

    def step(index, _):
        weight = 2.0 / (index.astype(jnp.float32) + 3.0)
        short = False

        blocks[me_b] = exact(ys[...], mixer[...], nt).astype(jnp.bfloat16)

        def own_copy(kind):
            target = (sibling, me_b + 2, me_b - 2)[kind]
            return remote(
                blocks.at[me_b], blocks.at[me_b], ag_send.at[kind], ag_recv.at[me_b], bucket=target
            )

        def go_on(b, d, step):
            return remote(
                blocks.at[b], blocks.at[b], line_send.at[d], ag_recv.at[b], bucket=me_b + step
            )

        def pass_on(b, d):
            return remote(blocks.at[b], blocks.at[b], fw_send.at[d], ag_recv.at[b], bucket=sibling)

        def arrival(b):
            return remote(
                blocks.at[b], blocks.at[b], ag_send.at[0], ag_recv.at[b], bucket=sibling
            )

        def product(b):
            return jnp.dot(
                pay_ref[0, :, columns(b)], blocks[b], preferred_element_type=jnp.float32
            )

        @pl.when(pair < pairs - 1)
        def _():
            own_copy(1).start()

        @pl.when(pair > 0)
        def _():
            own_copy(2).start()

        own_copy(0).start()
        @pl.when(index == 0)
        def _():
            def turn(j, _):
                pay_t[columns(j), :] = pay_ref[0, :, columns(j)].T
                return 0

            lax.fori_loop(0, n_b, turn, 0)
        grad[...] = product(me_b)
        arrival(sibling).wait_recv()
        grad[...] += product(sibling)

        def take(d, _):
            left = me_b - 2 * d
            right = me_b + 2 * d

            @pl.when(pair >= d)
            def _():
                arrival(left).wait_recv()

                @pl.when(pair < pairs - 1)
                def _():
                    go_on(left, d, 2).start()

                pass_on(left, d).start()

            @pl.when(pair + d < pairs)
            def _():
                arrival(right).wait_recv()

                @pl.when(pair > 0)
                def _():
                    go_on(right, pairs + d, -2).start()

                pass_on(right, pairs + d).start()

            def use(b, other):
                grad[...] += product(b)
                arrival(other).wait_recv()
                grad[...] += product(other)

            @pl.when(pair >= d)
            def _():
                use(left, sibling - 2 * d)

            @pl.when(pair + d < pairs)
            def _():
                use(right, sibling + 2 * d)

            return 0

        lax.fori_loop(1, pairs, take, 0)

        def drain(d, _):
            left = me_b - 2 * d
            right = me_b + 2 * d

            @pl.when(pair >= d)
            def _():
                pass_on(left, d).wait_send()

                @pl.when(pair < pairs - 1)
                def _():
                    go_on(left, d, 2).wait_send()

            @pl.when(pair + d < pairs)
            def _():
                pass_on(right, pairs + d).wait_send()

                @pl.when(pair > 0)
                def _():
                    go_on(right, pairs + d, -2).wait_send()

            return 0

        lax.fori_loop(1, pairs, drain, 0)
        own_copy(0).wait_send()

        @pl.when(pair < pairs - 1)
        def _():
            own_copy(1).wait_send()

        @pl.when(pair > 0)
        def _():
            own_copy(2).wait_send()

        prox(xs, -1.0, smooth_x, weight, short)

        mixed[...] = exact(xs[...], mixer[...]).astype(jnp.bfloat16)

        def partial(b):
            return jnp.dot(pay_t[columns(b), :], mixed[...], preferred_element_type=jnp.float32)

        def sib_copy(q):
            return remote(
                sib_out.at[q], sib_in.at[q], sib_send.at[q], sib_recv.at[q], bucket=sibling
            )

        def far_copy(q, step, target):
            slot = q if step > 0 else pairs + q
            if not short:
                return [
                    remote(
                        far_out.at[q],
                        far_in.at[slot],
                        far_send.at[q],
                        far_recv.at[slot],
                        bucket=target,
                    )
                ]
            return [
                remote(
                    far_q.at[q],
                    far_q_in.at[slot],
                    far_send.at[q],
                    far_recv.at[slot],
                    bucket=target,
                ),
                remote(
                    far_s.at[q],
                    far_s_in.at[slot],
                    far_s_send.at[q],
                    far_s_recv.at[slot],
                    bucket=target,
                ),
            ]

        def far_value(q, step):
            slot = q if step > 0 else pairs + q
            for copy in far_copy(q, step, sibling):
                copy.wait_recv()
            if short:
                return decoded(far_q_in.at[slot], far_s_in.at[slot])
            return far_in[slot]

        def to_sibling(q):
            sib_out[q] = partial(q * 2 + 1 - core)
            sib_copy(q).start()

        def move(q, step):
            far_out[q] = partial(q * 2 + core)
            sib_copy(q).wait_recv()
            far_out[q] += sib_in[q]

            @pl.when(pair > 0 if step > 0 else pair < pairs - 1)
            def _():
                far_out[q] += far_value(q, step)

            if short:
                coded(far_out[q], far_q.at[q], far_s.at[q])
            for copy in far_copy(q, step, me_b + step):
                copy.start()

        def outward(right, left):
            def one(i, _):
                @pl.when(pair < pairs - 1 - i)
                def _():
                    right(pairs - 1 - i)

                @pl.when(pair > i)
                def _():
                    left(i)

                return 0

            lax.fori_loop(0, pairs - 1, one, 0)

        def far_done(q, step):
            for copy in far_copy(q, step, me_b + step):
                copy.wait_send()

        outward(to_sibling, to_sibling)
        to_sibling(pair)
        outward(lambda q: move(q, 2), lambda q: move(q, -2))
        grad[...] = partial(me_b)
        sib_copy(pair).wait_recv()
        grad[...] += sib_in[pair]

        @pl.when(pair > 0)
        def _():
            grad[...] += far_value(pair, 2)

        @pl.when(pair < pairs - 1)
        def _():
            grad[...] += far_value(pair, -2)

        outward(lambda q: far_done(q, 2), lambda q: far_done(q, -2))
        for q in range(pairs):
            sib_copy(q).wait_send()
        prox(ys, 1.0, smooth_y, weight, short)
        return 0

    lax.fori_loop(0, 2, step, 0)
    down = lax.broadcasted_iota(jnp.int32, (seqs, seqs), 0)
    across = lax.broadcasted_iota(jnp.int32, (seqs, seqs), 1)
    to_outer = (order(down) == across).astype(jnp.float32)
    xo_ref[0] = exact(xs[...], to_outer)
    yo_ref[0] = exact(ys[...], to_outer)


def body(x_start, y_start, bucket_payoff, column_blocks, public_coef, predecessor_sequences):
    n_r = lax.axis_size("round")
    n_b = lax.axis_size("bucket")
    _, rows, seqs = x_start.shape
    part = rows // n_r
    pairs = n_b // 2
    f32, bf16 = jnp.float32, jnp.bfloat16
    vmem = pl.BlockSpec(memory_space=pltpu.VMEM)
    smem = pl.BlockSpec(memory_space=pltpu.SMEM)
    dma = pltpu.SemaphoreType.DMA
    return pl.pallas_call(
        functools.partial(kernel, n_r, n_b),
        out_shape=[jax.ShapeDtypeStruct(x_start.shape, f32)] * 2,
        in_specs=[vmem, vmem, vmem, smem, vmem, vmem],
        out_specs=[vmem, vmem],
        scratch_shapes=[
            pltpu.VMEM((rows, seqs), f32),
            pltpu.VMEM((rows, seqs), f32),
            pltpu.VMEM((seqs, seqs), f32),
            pltpu.VMEM((n_r - 1, seqs, seqs // 2), f32),
            pltpu.VMEM((n_b * rows, rows), bf16),
            pltpu.VMEM((n_b, rows, seqs), bf16),
            pltpu.VMEM((rows, seqs), bf16),
            pltpu.VMEM((rows, seqs), f32),
            pltpu.VMEM((pairs, rows, seqs), f32),
            pltpu.VMEM((pairs, rows, seqs), f32),
            pltpu.VMEM((pairs, rows, seqs), f32),
            pltpu.VMEM((2 * pairs, rows, seqs), f32),
            pltpu.VMEM((n_b, 8, 128), f32),
            pltpu.VMEM((n_r, 8, 128), f32),
            pltpu.VMEM((n_r, part, seqs), f32),
            pltpu.VMEM((n_r, part, seqs), f32),
            pltpu.VMEM((n_r, part, seqs // 2), f32),
            pltpu.VMEM((n_r, part, seqs), f32),
            pltpu.VMEM((n_r, part, seqs), f32),
            pltpu.VMEM((16, 128), jnp.int16),
            pltpu.VMEM((pairs, 8, seqs), f32),
            pltpu.VMEM((16, 128), jnp.int16),
            pltpu.VMEM((2 * pairs, 8, seqs), f32),
            pltpu.VMEM((16, 128), jnp.int16),
            pltpu.VMEM((n_r, 8, seqs), f32),
            pltpu.VMEM((16, 128), jnp.int16),
            pltpu.VMEM((n_r, 8, seqs), f32),
            pltpu.VMEM((16, 128), jnp.int16),
            pltpu.VMEM((n_r, 8, seqs), f32),
            pltpu.VMEM((16, 128), jnp.int16),
            pltpu.VMEM((n_r, 8, seqs), f32),
            dma((3,)),
            dma((n_b,)),
            dma((2 * pairs,)),
            dma((2 * pairs,)),
            dma((pairs,)),
            dma((pairs,)),
            dma((pairs,)),
            dma((2 * pairs,)),
            dma((n_b,)),
            dma((n_b,)),
            dma((n_r,)),
            dma((n_r,)),
            dma((n_r,)),
            dma((n_r,)),
            dma((n_r,)),
            dma((n_r,)),
            dma((pairs,)),
            dma((2 * pairs,)),
            dma((n_r,)),
            dma((n_r,)),
            dma((n_r,)),
            dma((n_r,)),
        ],
        compiler_params=pltpu.CompilerParams(
            collective_id=0, has_side_effects=True, vmem_limit_bytes=60 * 1024 * 1024
        ),
    )(x_start, y_start, bucket_payoff, column_blocks, public_coef, predecessor_sequences)


def solution(mesh):
    in_specs = (
        P("round", "bucket", None),
        P("round", "bucket", None),
        P("round", "bucket", None),
        P("round", None, None),
        P("round", None, None, None, None),
        P(),
    )
    out_specs = (P("round", "bucket", None), P("round", "bucket", None))

    def run(*arrays):
        return tuple(
            jax.shard_map(
                body, mesh=mesh, in_specs=in_specs, out_specs=out_specs, check_vma=False
            )(*arrays)
        )

    return run
```
